32 devices in a mesh: groups: 2 (over x), ao: 16 (over z, y, core).
Axes of the slice: x: 2, y: 2, z: 4, core: 2. Of those that a mesh axis runs over, the one named last changes fastest.
Arguments:
- b_factor: bfloat16 [512, 4, 8192], P('ao', 'groups'), parts along dimension 1, may hold values from -2.5 to 2.5
- tile_pairs: int32 [512, 2], P(('groups', 'ao')), parts along dimension 0, may hold values from 0 to 63, as said below
- tile_count: int32 [32], P(('groups', 'ao')), parts along dimension 0, may hold values from 3 to 16, as said below
Outputs:
- k_tiles: float32 [512, 128, 128], P(('groups', 'ao')), parts along dimension 0
The draws below stay inside these ranges and needn't reach their ends.
There are 2 independent parts, one for each index of `groups`. The reference program is written for one: setup_inputs(seed, part) draws one part's arguments, and reference() takes and returns one part's arrays. A program takes and returns all parts, laid end to end along the dimension named above; each array names one. Nothing has to cross between parts.
Inputs may be any that keep to these rules, and one draw needn't show every extreme that they name: `tile_pairs`: each row names a row block no larger than its column block. The live rows of a device name exactly 6 distinct blocks; the live rows of devices 2k and 2k+1 together name 10 consecutive blocks. Rows that are not live also hold valid block numbers. `tile_count`: some device fills all 16 slots.
All inputs are finite; a program needn't handle non-finite values.
Results may differ from the reference program's by a relative error of at most 0.0003.
Values may be sent and summed in bfloat16 or wider, within the bound.
A program may use at most 64 MiB of HBM per device.

```python
import jax
import jax.numpy as jnp
import numpy as np
from jax import lax

NAO = 8192
NOCC = 512
AUX = 2
BLK = 128
SLOTS = 16
NEED = 6
WINDOW = 10
N_AO = 16


def label_table(label_count):
    covering = [(i, i + 1) for i in range(0, label_count, 2)]
    remaining = [(i, j) for i in range(label_count) for j in range(i, label_count) if (i, j) not in covering]
    return np.array(covering + remaining, dtype=np.int32)


def pair_tiles(tile_key, labels, label_pairs, covered):
    spare_count = label_pairs.shape[0] - covered
    ordering = jax.random.permutation(tile_key, spare_count)[:SLOTS - covered].astype(jnp.int32) + covered
    position_list = jnp.concatenate([jnp.arange(covered, dtype=jnp.int32), ordering])
    chosen = jnp.asarray(label_pairs)[position_list]
    named_blocks = labels[chosen]
    return jnp.stack([jnp.min(named_blocks, axis=1), jnp.max(named_blocks, axis=1)], axis=1)


def draw_tile_pairs(key, part):
    key = jax.random.fold_in(key, 11)
    label_pairs = label_table(NEED)
    covered = NEED // 2
    block_total = NAO // BLK

    def one_couple(couple_key):
        head_key, middle_key, even_key, odd_key = jax.random.split(couple_key, 4)
        window_start = jax.random.randint(head_key, (), 0, block_total - WINDOW + 1).astype(jnp.int32)
        middle = jax.random.permutation(middle_key, WINDOW - 2).astype(jnp.int32) + window_start + 1
        window_head = jnp.reshape(window_start, (1,))
        window_end = jnp.reshape(window_start + WINDOW - 1, (1,))
        even_labels = jnp.concatenate([window_head, middle[:NEED - 2], window_end])
        odd_labels = jnp.concatenate([window_head, middle[NEED - 2:], window_end])
        return jnp.stack([pair_tiles(even_key, even_labels, label_pairs, covered), pair_tiles(odd_key, odd_labels, label_pairs, covered)])
    couples = jax.vmap(one_couple)(jax.random.split(key, N_AO // 2))
    return couples.reshape(N_AO * SLOTS, 2).astype(jnp.int32)


def draw_tile_count(key, part):
    key = jax.random.fold_in(key, 23)
    busy_key, drawn_key, pick_key = jax.random.split(key, 3)
    drawn_count = jax.random.randint(drawn_key, (N_AO,), NEED // 2, NEED // 2 + 6)
    chosen = jax.random.randint(pick_key, (), 0, N_AO)
    busy_flag = (jax.random.randint(busy_key, (N_AO,), 0, 8) == 0) | (jnp.arange(N_AO) == chosen)
    return jnp.where(busy_flag, SLOTS, drawn_count).astype(jnp.int32)


def level_of(key, shape, shards, low, high):
    gain = 1.0
    for dim, shards_of in shards:
        heights = jax.random.uniform(jax.random.fold_in(jax.random.fold_in(key, 6), dim), (shards_of,), jnp.float32, low / len(shards), high / len(shards))
        gain = gain * jnp.repeat(jnp.exp(heights), shape[dim] // shards_of).reshape((-1,) + (1,) * (len(shape) - 1 - dim))
    return gain


def centred(key, shape, deviation, reach, pieces=(), kind=jnp.bfloat16):
    entries = deviation * jax.random.normal(key, shape, jnp.float32)
    if pieces:
        entries = entries * level_of(key, shape, pieces, -0.22, 0.18)
    return jnp.clip(entries, -reach, reach).astype(kind)


def setup_inputs(seed: int = 0, part: int = 0) -> dict:
    key_of = jax.random.split(jax.random.key(seed), 4)
    own_keys = jax.random.split(jax.random.fold_in(key_of[3], part), 4)
    b_factor = centred(own_keys[0], (NOCC, AUX, NAO), ((NOCC * AUX) ** -0.25), 2.5, ((0, 16),))
    tile_pairs = draw_tile_pairs(jax.random.fold_in(jax.random.fold_in(key_of[3], part), 71), part)
    tile_count = draw_tile_count(jax.random.fold_in(jax.random.fold_in(key_of[3], part), 71), part)
    return {"b_factor": b_factor, "tile_pairs": tile_pairs, "tile_count": tile_count}


def reference(b_factor, tile_pairs, tile_count):
    occupied, auxiliary, orbitals = b_factor.shape
    flattened = b_factor.reshape(occupied * auxiliary, orbitals)
    rows_all = jnp.arange(N_AO * SLOTS, dtype=jnp.int32)
    live_flags = (rows_all % SLOTS) < tile_count[rows_all // SLOTS]

    def compute(tile_pair):
        left_block = lax.dynamic_slice_in_dim(flattened, (tile_pair[0] * BLK).astype(jnp.int32), BLK, 1)
        right_block = lax.dynamic_slice_in_dim(flattened, (tile_pair[1] * BLK).astype(jnp.int32), BLK, 1)
        return lax.dot_general(left_block, right_block, (((0,), (0,)), ((), ())), preferred_element_type=jnp.float32)

    def nothing(tile_pair):
        return jnp.zeros((BLK, BLK), jnp.float32)

    def one_tile(operands):
        tile_pair, live_flag = operands
        return lax.cond(live_flag, compute, nothing, tile_pair)

    return lax.map(one_tile, (tile_pairs, live_flags))
```

```python
import functools

import jax
import jax.numpy as jnp
from jax import lax
from jax.experimental import pallas as pl
from jax.experimental.pallas import tpu as pltpu
from jax.sharding import PartitionSpec as P

BLK = 128
WINDOW = 10
HALF = WINDOW // 2
MESH = pl.DeviceIdType.MESH


def partner(chip, offset):
    bit = 1
    while bit <= offset:
        if offset & bit:
            chip = chip + bit - 2 * bit * (chip // bit % 2)
        bit *= 2
    return chip


def phase_lists(chips):
    far = list(range(chips - 1, 0, -1))
    return [[0] + far]


def kernel(chips, phases, pairs_ref, count_ref, b_ref, out_ref, note, notes, send, *rest):
    recvs = rest[:len(phases)]
    note_send, note_recv, data_send, data_recv, pass_send, pass_recv = rest[len(phases):]
    me = lax.axis_index("ao")
    chip, core = me // 2, me % 2
    sibling = me + 1 - 2 * core
    devices = 2 * chips
    slots = pairs_ref.shape[0]
    block_total = b_ref.shape[0]
    where_of = {d: (p, i) for p, group in enumerate(phases) for i, d in enumerate(group)}

    barrier = pltpu.get_barrier_semaphore()

    def greet(step, carry):
        other = lax.rem(me + step, devices)
        pl.semaphore_signal(barrier, inc=1, device_id={"ao": other}, device_id_type=MESH)
        return carry

    lax.fori_loop(1, devices, greet, 0)

    count = count_ref[0]
    lowest = jnp.int32(block_total - WINDOW)
    for t in range(slots):
        lowest = jnp.minimum(lowest, jnp.where(t < count, pairs_ref[t, 0], block_total - WINDOW))
    note[...] = jnp.full(note.shape, lowest, jnp.int32)
    notes[me] = note[...]
    pl.semaphore_wait(barrier, devices - 1)

    def note_copy(step, sender):
        other = lax.rem(me + step, devices)
        return pltpu.make_async_remote_copy(
            src_ref=note, dst_ref=notes.at[sender], send_sem=note_send.at[step],
            recv_sem=note_recv.at[step], device_id={"ao": other}, device_id_type=MESH)

    def start_note(step, carry):
        note_copy(step, me).start()
        return carry

    def end_note(step, carry):
        sender = lax.rem(me + devices - step, devices)
        note_copy(step, sender).wait_recv()
        return carry

    def end_note_send(step, carry):
        note_copy(step, me).wait_send()
        return carry

    lax.fori_loop(1, devices, start_note, 0)
    lax.fori_loop(1, devices, end_note, 0)

    def window_of(which):
        return jnp.maximum(jnp.min(notes[pl.ds(2 * which, 2)]), 0)

    def data_copy(d, sender_core, c):
        p, i = where_of[d]
        return pltpu.make_async_remote_copy(
            src_ref=send.at[d, c], dst_ref=recvs[p].at[i, sender_core, pl.ds(HALF * c, HALF)],
            send_sem=data_send.at[d, c], recv_sem=data_recv.at[d, sender_core],
            device_id={"ao": 2 * partner(chip, d) + c}, device_id_type=MESH)

    def pass_copy(d, s, c):
        p, i = where_of[d]
        part = recvs[p].at[i, s, pl.ds(HALF * c, HALF)]
        return pltpu.make_async_remote_copy(
            src_ref=part, dst_ref=part, send_sem=pass_send.at[d, s], recv_sem=pass_recv.at[d, s],
            device_id={"ao": sibling}, device_id_type=MESH)

    order = [d for group in phases for d in group if d]
    for d in order:
        low = window_of(partner(chip, d))
        for c in range(2):
            send[d, c] = b_ref[pl.ds(low + HALF * c, HALF)]
            data_copy(d, core, c).start()

    my_low = window_of(chip)
    p0, i0 = where_of[0]
    recvs[p0][i0, core] = b_ref[pl.ds(my_low, WINDOW)]

    def own_copy(s):
        part = recvs[p0].at[i0, s]
        return pltpu.make_async_remote_copy(
            src_ref=part, dst_ref=part, send_sem=pass_send.at[0, 0], recv_sem=pass_recv.at[0, 0],
            device_id={"ao": sibling}, device_id_type=MESH)

    own_copy(core).start()
    for d in order:
        for s in range(2):
            data_copy(d, s, core).wait_recv()
            pass_copy(d, s, core).start()

    for p, group in enumerate(phases):
        for d in group:
            if d == 0:
                own_copy(1 - core).wait_recv()
            else:
                for s in range(2):
                    pass_copy(d, s, 1 - core).wait_recv()

        def tile(t, carry):
            left = jnp.clip(pairs_ref[t, 0] - my_low, 0, WINDOW - 1)
            right = jnp.clip(pairs_ref[t, 1] - my_low, 0, WINDOW - 1)
            a = recvs[p][:, :, left].reshape(-1, BLK)
            b = recvs[p][:, :, right].reshape(-1, BLK)
            value = lax.dot_general(a, b, (((0,), (0,)), ((), ())), preferred_element_type=jnp.float32)
            if p:
                value = value + out_ref[t]
            if p == len(phases) - 1:
                value = jnp.where(t < count, value, 0.0)
            out_ref[t] = value
            return carry

        lax.fori_loop(0, slots, tile, 0)

    lax.fori_loop(1, devices, end_note_send, 0)
    own_copy(core).wait_send()
    for d in order:
        for c in range(2):
            data_copy(d, core, c).wait_send()
            pass_copy(d, c, core).wait_send()


def shards(b_factor, tile_pairs, tile_count):
    devices = lax.axis_size("ao")
    chips = devices // 2
    occ_local, auxiliary, orbitals = b_factor.shape
    depth = occ_local * auxiliary
    block_total = orbitals // BLK
    slots = tile_pairs.shape[0]
    blocks = b_factor.reshape(depth, block_total, BLK).transpose(1, 0, 2)
    phases = phase_lists(chips)
    return pl.pallas_call(
        functools.partial(kernel, chips, phases),
        out_shape=jax.ShapeDtypeStruct((slots, BLK, BLK), jnp.float32),
        in_specs=[
            pl.BlockSpec(memory_space=pltpu.SMEM),
            pl.BlockSpec(memory_space=pltpu.SMEM),
            pl.BlockSpec(memory_space=pltpu.VMEM),
        ],
        out_specs=pl.BlockSpec(memory_space=pltpu.VMEM),
        scratch_shapes=[
            pltpu.VMEM((8, BLK), jnp.int32),
            pltpu.VMEM((devices, 8, BLK), jnp.int32),
            pltpu.VMEM((chips, 2, HALF, depth, BLK), jnp.bfloat16),
            *[pltpu.VMEM((len(group), 2, WINDOW, depth, BLK), jnp.bfloat16) for group in phases],
            pltpu.SemaphoreType.DMA((devices,)),
            pltpu.SemaphoreType.DMA((devices,)),
            pltpu.SemaphoreType.DMA((chips, 2)),
            pltpu.SemaphoreType.DMA((chips, 2)),
            pltpu.SemaphoreType.DMA((chips, 2)),
            pltpu.SemaphoreType.DMA((chips, 2)),
        ],
        compiler_params=pltpu.CompilerParams(
            collective_id=0, has_side_effects=True, vmem_limit_bytes=32 * 1024 * 1024),
    )(tile_pairs, tile_count, blocks)


def solution(mesh):
    in_specs = (P("ao", "groups", None), P(("groups", "ao"), None), P(("groups", "ao")))
    out_specs = P(("groups", "ao"), None, None)
    return jax.shard_map(shards, mesh=mesh, in_specs=in_specs, out_specs=out_specs, check_vma=False)
```

```python
import functools

import jax
import jax.numpy as jnp
from jax import lax
from jax.experimental import pallas as pl
from jax.experimental.pallas import tpu as pltpu
from jax.sharding import PartitionSpec as P

BLK = 128
WINDOW = 10
HALF = WINDOW // 2
MESH = pl.DeviceIdType.MESH


def partner(chip, offset):
    bit = 1
    while bit <= offset:
        if offset & bit:
            chip = chip + bit - 2 * bit * (chip // bit % 2)
        bit *= 2
    return chip


def phase_lists(chips):
    half = chips // 2
    quarter = half // 2
    first = [0, half + quarter] + list(range(1, half))
    return [first, [d for d in range(half, chips) if d not in first]]


def kernel(chips, phases, pairs_ref, count_ref, b_ref, out_ref, note, notes, send, *rest):
    recvs = rest[:len(phases)]
    note_send, note_recv, data_send, data_recv, pass_send, pass_recv = rest[len(phases):]
    me = lax.axis_index("ao")
    chip, core = me // 2, me % 2
    sibling = me + 1 - 2 * core
    devices = 2 * chips
    slots = pairs_ref.shape[1]
    block_total = b_ref.shape[0]
    where_of = {d: (p, i) for p, group in enumerate(phases) for i, d in enumerate(group)}

    barrier = pltpu.get_barrier_semaphore()

    def greet(step, carry):
        other = lax.rem(me + step, devices)
        pl.semaphore_signal(barrier, inc=1, device_id={"ao": other}, device_id_type=MESH)
        return carry

    lax.fori_loop(1, devices, greet, 0)

    count = count_ref[0]
    lowest = jnp.int32(block_total - WINDOW)
    for t in range(slots):
        lowest = jnp.minimum(lowest, jnp.where(t < count, pairs_ref[0, t], block_total - WINDOW))
    note[...] = jnp.full(note.shape, lowest, jnp.int32)
    notes[me] = note[...]
    pl.semaphore_wait(barrier, devices - 1)

    order = [d for group in phases for d in group if d]
    peers = [(d, c) for d in order for c in range(2)]

    def note_copy(d, c, sender):
        return pltpu.make_async_remote_copy(
            src_ref=note, dst_ref=notes.at[sender], send_sem=note_send.at[d, c],
            recv_sem=note_recv.at[d, sender % 2], device_id={"ao": 2 * partner(chip, d) + c},
            device_id_type=MESH)

    def sibling_note(sender):
        return pltpu.make_async_remote_copy(
            src_ref=note, dst_ref=notes.at[sender], send_sem=note_send.at[0, 0],
            recv_sem=note_recv.at[0, 0], device_id={"ao": sibling}, device_id_type=MESH)

    for d, c in peers:
        note_copy(d, c, me).start()
    sibling_note(me).start()

    def window_of(which):
        return jnp.maximum(jnp.min(notes[pl.ds(2 * which, 2)]), 0)

    def data_copy(d, sender_core, c):
        p, i = where_of[d]
        return pltpu.make_async_remote_copy(
            src_ref=send.at[d, c], dst_ref=recvs[p].at[i, sender_core, pl.ds(HALF * c, HALF)],
            send_sem=data_send.at[d, c], recv_sem=data_recv.at[d, sender_core],
            device_id={"ao": 2 * partner(chip, d) + c}, device_id_type=MESH)

    def pass_copy(d, s, c):
        p, i = where_of[d]
        part = recvs[p].at[i, s, pl.ds(HALF * c, HALF)]
        return pltpu.make_async_remote_copy(
            src_ref=part, dst_ref=part, send_sem=pass_send.at[d, s], recv_sem=pass_recv.at[d, s],
            device_id={"ao": sibling}, device_id_type=MESH)

    for d in order:
        for c in range(2):
            note_copy(d, c, 2 * partner(chip, d) + c).wait_recv()
        low = window_of(partner(chip, d))
        for c in range(2):
            send[d, c] = b_ref[pl.ds(low + HALF * c, HALF)]
            data_copy(d, core, c).start()

    sibling_note(sibling).wait_recv()
    my_low = window_of(chip)
    p0, i0 = where_of[0]
    recvs[p0][i0, core] = b_ref[pl.ds(my_low, WINDOW)]

    def own_copy(s):
        part = recvs[p0].at[i0, s]
        return pltpu.make_async_remote_copy(
            src_ref=part, dst_ref=part, send_sem=pass_send.at[0, 0], recv_sem=pass_recv.at[0, 0],
            device_id={"ao": sibling}, device_id_type=MESH)

    own_copy(core).start()

    def pass_on(p):
        for d in phases[p]:
            for s in range(2):
                if d:
                    data_copy(d, s, core).wait_recv()
                    pass_copy(d, s, core).start()

    def multiply(p):
        for d in phases[p]:
            if d == 0:
                own_copy(1 - core).wait_recv()
            else:
                for s in range(2):
                    pass_copy(d, s, 1 - core).wait_recv()

        def tile(t):
            left = jnp.clip(pairs_ref[0, t] - my_low, 0, WINDOW - 1)
            right = jnp.clip(pairs_ref[1, t] - my_low, 0, WINDOW - 1)
            a = recvs[p][:, :, left].reshape(-1, BLK)
            b = recvs[p][:, :, right].reshape(-1, BLK)
            value = lax.dot_general(a, b, (((0,), (0,)), ((), ())), preferred_element_type=jnp.float32)
            if p:
                value = value + out_ref[t]
            if p == len(phases) - 1:
                value = jnp.where(t < count, value, 0.0)
            out_ref[t] = value

        for t in range(slots):
            tile(t)

    pass_on(0)
    for p in range(1, len(phases)):
        pass_on(p)
        multiply(p - 1)
    multiply(len(phases) - 1)

    sibling_note(me).wait_send()
    for d, c in peers:
        note_copy(d, c, me).wait_send()
    own_copy(core).wait_send()
    for d in order:
        for c in range(2):
            data_copy(d, core, c).wait_send()
            pass_copy(d, c, core).wait_send()


def shards(b_factor, tile_pairs, tile_count):
    devices = lax.axis_size("ao")
    chips = devices // 2
    occ_local, auxiliary, orbitals = b_factor.shape
    depth = occ_local * auxiliary
    block_total = orbitals // BLK
    slots = tile_pairs.shape[0]
    blocks = b_factor.reshape(depth, block_total, BLK).transpose(1, 0, 2)
    phases = phase_lists(chips)
    return pl.pallas_call(
        functools.partial(kernel, chips, phases),
        out_shape=jax.ShapeDtypeStruct((slots, BLK, BLK), jnp.float32),
        in_specs=[
            pl.BlockSpec(memory_space=pltpu.SMEM),
            pl.BlockSpec(memory_space=pltpu.SMEM),
            pl.BlockSpec(memory_space=pltpu.VMEM),
        ],
        out_specs=pl.BlockSpec(memory_space=pltpu.VMEM),
        scratch_shapes=[
            pltpu.VMEM((1, BLK), jnp.int32),
            pltpu.VMEM((devices, 1, BLK), jnp.int32),
            pltpu.VMEM((chips, 2, HALF, depth, BLK), jnp.bfloat16),
            *[pltpu.VMEM((len(group), 2, WINDOW, depth, BLK), jnp.bfloat16) for group in phases],
            pltpu.SemaphoreType.DMA((chips, 2)),
            pltpu.SemaphoreType.DMA((chips, 2)),
            pltpu.SemaphoreType.DMA((chips, 2)),
            pltpu.SemaphoreType.DMA((chips, 2)),
            pltpu.SemaphoreType.DMA((chips, 2)),
            pltpu.SemaphoreType.DMA((chips, 2)),
        ],
        compiler_params=pltpu.CompilerParams(
            collective_id=0, has_side_effects=True, vmem_limit_bytes=32 * 1024 * 1024),
    )(tile_pairs.T, tile_count, blocks)


def solution(mesh):
    in_specs = (P("ao", "groups", None), P(("groups", "ao"), None), P(("groups", "ao")))
    out_specs = P(("groups", "ao"), None, None)
    return jax.shard_map(shards, mesh=mesh, in_specs=in_specs, out_specs=out_specs, check_vma=False)
```

```python
import functools

import jax
import jax.numpy as jnp
from jax import lax
from jax.experimental import pallas as pl
from jax.experimental.pallas import tpu as pltpu
from jax.sharding import PartitionSpec as P

BLK = 128
WINDOW = 10
HALF = WINDOW // 2
MESH = pl.DeviceIdType.MESH


def partner(chip, offset):
    bit = 1
    while bit <= offset:
        if offset & bit:
            chip = chip + bit - 2 * bit * (chip // bit % 2)
        bit *= 2
    return chip


def phase_lists(chips):
    half, quarter = chips // 2, chips // 4
    first = [0, half + quarter] + list(range(1, half + 1))
    return [first, [d for d in range(half, chips) if d not in first]]


def kernel(chips, phases, pairs_hbm, count_hbm, b_hbm, out_ref, pairs_ref, count_ref, raw, b_ref, note, notes, send, *rest):
    recvs = rest[:len(phases)]
    small_sem, raw_sem, note_send, note_recv, data_send, data_recv, pass_send, pass_recv = rest[len(phases):]
    me = lax.axis_index("ao")
    chip, core = me // 2, me % 2
    sibling = me + 1 - 2 * core
    devices = 2 * chips
    slots = pairs_ref.shape[1]
    block_total = b_ref.shape[0]
    where_of = {d: (p, i) for p, group in enumerate(phases) for i, d in enumerate(group)}

    small = [
        pltpu.make_async_copy(pairs_hbm, pairs_ref, small_sem.at[0]),
        pltpu.make_async_copy(count_hbm, count_ref, small_sem.at[1]),
    ]
    for copy in small:
        copy.start()
    barrier = pltpu.get_barrier_semaphore()

    def greet(step, carry):
        other = lax.rem(me + step, devices)
        pl.semaphore_signal(barrier, inc=1, device_id={"ao": other}, device_id_type=MESH)
        return carry

    lax.fori_loop(1, devices, greet, 0)
    fetch = pltpu.make_async_copy(b_hbm, raw, raw_sem)
    fetch.start()

    for copy in small:
        copy.wait()
    count = count_ref[0]
    lowest = jnp.int32(block_total - WINDOW)
    for t in range(slots):
        lowest = jnp.minimum(lowest, jnp.where(t < count, pairs_ref[0, t], block_total - WINDOW))
    note[...] = jnp.full(note.shape, lowest, jnp.int32)
    notes[me] = note[...]
    pl.semaphore_wait(barrier, devices - 1)

    order = [d for group in phases for d in group if d]
    peers = [(d, c) for d in order for c in range(2)]

    def note_copy(d, c, sender):
        return pltpu.make_async_remote_copy(
            src_ref=note, dst_ref=notes.at[sender], send_sem=note_send.at[d, c],
            recv_sem=note_recv.at[d, sender % 2], device_id={"ao": 2 * partner(chip, d) + c},
            device_id_type=MESH)

    def sibling_note(sender):
        return pltpu.make_async_remote_copy(
            src_ref=note, dst_ref=notes.at[sender], send_sem=note_send.at[0, 0],
            recv_sem=note_recv.at[0, 0], device_id={"ao": sibling}, device_id_type=MESH)

    for d, c in peers:
        note_copy(d, c, me).start()
    sibling_note(me).start()

    fetch.wait()
    for j in range(block_total):
        b_ref[j] = raw[:, :, BLK * j:BLK * (j + 1)].reshape(b_ref.shape[1:])

    def window_of(which):
        return jnp.maximum(jnp.min(notes[pl.ds(2 * which, 2)]), 0)

    def data_copy(d, sender_core, c):
        p, i = where_of[d]
        return pltpu.make_async_remote_copy(
            src_ref=send.at[d, c], dst_ref=recvs[p].at[i, sender_core, pl.ds(HALF * c, HALF)],
            send_sem=data_send.at[d, c], recv_sem=data_recv.at[d, sender_core],
            device_id={"ao": 2 * partner(chip, d) + c}, device_id_type=MESH)

    def pass_copy(d, s, c):
        p, i = where_of[d]
        part = recvs[p].at[i, s, pl.ds(HALF * c, HALF)]
        return pltpu.make_async_remote_copy(
            src_ref=part, dst_ref=part, send_sem=pass_send.at[d, s], recv_sem=pass_recv.at[d, s],
            device_id={"ao": sibling}, device_id_type=MESH)

    for d in order:
        for c in range(2):
            note_copy(d, c, 2 * partner(chip, d) + c).wait_recv()
        low = window_of(partner(chip, d))
        for c in range(2):
            send[d, c] = b_ref[pl.ds(low + HALF * c, HALF)]
            data_copy(d, core, c).start()

    sibling_note(sibling).wait_recv()
    my_low = window_of(chip)
    p0, i0 = where_of[0]
    recvs[p0][i0, core] = b_ref[pl.ds(my_low, WINDOW)]

    def own_copy(s):
        part = recvs[p0].at[i0, s]
        return pltpu.make_async_remote_copy(
            src_ref=part, dst_ref=part, send_sem=pass_send.at[0, 0], recv_sem=pass_recv.at[0, 0],
            device_id={"ao": sibling}, device_id_type=MESH)

    own_copy(core).start()

    def pass_on(p):
        for d in phases[p]:
            for s in range(2):
                if d:
                    data_copy(d, s, core).wait_recv()
                    pass_copy(d, s, core).start()

    def multiply(p):
        for d in phases[p]:
            if d == 0:
                own_copy(1 - core).wait_recv()
            else:
                for s in range(2):
                    pass_copy(d, s, 1 - core).wait_recv()

        def tile(t):
            left = jnp.clip(pairs_ref[0, t] - my_low, 0, WINDOW - 1)
            right = jnp.clip(pairs_ref[1, t] - my_low, 0, WINDOW - 1)
            a = recvs[p][:, :, left].reshape(-1, BLK)
            b = recvs[p][:, :, right].reshape(-1, BLK)
            value = lax.dot_general(a, b, (((0,), (0,)), ((), ())), preferred_element_type=jnp.float32)
            if p:
                value = value + out_ref[t]
            if p == len(phases) - 1:
                value = jnp.where(t < count, value, 0.0)
            out_ref[t] = value

        for t in range(slots):
            tile(t)

    pass_on(0)
    for p in range(1, len(phases)):
        pass_on(p)
        multiply(p - 1)
    multiply(len(phases) - 1)

    sibling_note(me).wait_send()
    for d, c in peers:
        note_copy(d, c, me).wait_send()
    own_copy(core).wait_send()
    for d in order:
        for c in range(2):
            data_copy(d, core, c).wait_send()
            pass_copy(d, c, core).wait_send()


def shards(b_factor, tile_pairs, tile_count):
    devices = lax.axis_size("ao")
    chips = devices // 2
    occ_local, auxiliary, orbitals = b_factor.shape
    depth = occ_local * auxiliary
    block_total = orbitals // BLK
    slots = tile_pairs.shape[0]
    phases = phase_lists(chips)
    return pl.pallas_call(
        functools.partial(kernel, chips, phases),
        out_shape=jax.ShapeDtypeStruct((slots, BLK, BLK), jnp.float32),
        in_specs=[
            pl.BlockSpec(memory_space=pltpu.HBM),
            pl.BlockSpec(memory_space=pltpu.HBM),
            pl.BlockSpec(memory_space=pltpu.HBM),
        ],
        out_specs=pl.BlockSpec(memory_space=pltpu.VMEM),
        scratch_shapes=[
            pltpu.SMEM((2, slots), jnp.int32),
            pltpu.SMEM((1,), jnp.int32),
            pltpu.VMEM(b_factor.shape, jnp.bfloat16),
            pltpu.VMEM((block_total, depth, BLK), jnp.bfloat16),
            pltpu.VMEM((1, BLK), jnp.int32),
            pltpu.VMEM((devices, 1, BLK), jnp.int32),
            pltpu.VMEM((chips, 2, HALF, depth, BLK), jnp.bfloat16),
            *[pltpu.VMEM((len(group), 2, WINDOW, depth, BLK), jnp.bfloat16) for group in phases],
            pltpu.SemaphoreType.DMA((2,)),
            pltpu.SemaphoreType.DMA,
            pltpu.SemaphoreType.DMA((chips, 2)),
            pltpu.SemaphoreType.DMA((chips, 2)),
            pltpu.SemaphoreType.DMA((chips, 2)),
            pltpu.SemaphoreType.DMA((chips, 2)),
            pltpu.SemaphoreType.DMA((chips, 2)),
            pltpu.SemaphoreType.DMA((chips, 2)),
        ],
        compiler_params=pltpu.CompilerParams(
            collective_id=0, has_side_effects=True, vmem_limit_bytes=60 * 1024 * 1024),
    )(tile_pairs.T, tile_count, b_factor)


def solution(mesh):
    in_specs = (P("ao", "groups", None), P(("groups", "ao"), None), P(("groups", "ao")))
    out_specs = P(("groups", "ao"), None, None)
    return jax.shard_map(shards, mesh=mesh, in_specs=in_specs, out_specs=out_specs, check_vma=False)
```

```python
import functools

import jax
import jax.numpy as jnp
from jax import lax
from jax.experimental import pallas as pl
from jax.experimental.pallas import tpu as pltpu
from jax.sharding import PartitionSpec as P

BLK = 128
WINDOW = 10
HALF = WINDOW // 2
MESH = pl.DeviceIdType.MESH


def partner(chip, offset):
    bit = 1
    while bit <= offset:
        if offset & bit:
            chip = chip + bit - 2 * bit * (chip // bit % 2)
        bit *= 2
    return chip


def phase_lists(chips):
    half, quarter = chips // 2, chips // 4
    first = [0, half + quarter] + list(range(1, half + 1))
    return [first, [d for d in range(half, chips) if d not in first]]


def kernel(chips, phases, pairs_hbm, count_ref, b_hbm, out_ref, pairs_ref, raw, b_ref, note, notes, send, *rest):
    recvs = rest[:len(phases)]
    small_sem, raw_sem, note_send, note_recv, data_send, data_recv, pass_send, pass_recv = rest[len(phases):]
    me = lax.axis_index("ao")
    chip, core = me // 2, me % 2
    sibling = me + 1 - 2 * core
    devices = 2 * chips
    slots = pairs_ref.shape[1]
    block_total = b_ref.shape[0]
    where_of = {d: (p, i) for p, group in enumerate(phases) for i, d in enumerate(group)}

    small = pltpu.make_async_copy(pairs_hbm, pairs_ref, small_sem)
    small.start()
    barrier = pltpu.get_barrier_semaphore()

    def greet(step, carry):
        other = lax.rem(me + step, devices)
        pl.semaphore_signal(barrier, inc=1, device_id={"ao": other}, device_id_type=MESH)
        return carry

    lax.fori_loop(1, devices, greet, 0)
    fetch = pltpu.make_async_copy(b_hbm, raw, raw_sem)
    fetch.start()

    small.wait()
    count = count_ref[0]
    lowest = jnp.int32(block_total - WINDOW)
    for t in range(slots):
        lowest = jnp.minimum(lowest, jnp.where(t < count, pairs_ref[0, t], block_total - WINDOW))
    note[...] = jnp.full(note.shape, lowest, jnp.int32)
    notes[me] = note[...]
    pl.semaphore_wait(barrier, devices - 1)

    order = [d for group in phases for d in group if d]
    peers = [(d, c) for d in order for c in range(2)]

    def note_copy(d, c, sender):
        return pltpu.make_async_remote_copy(
            src_ref=note, dst_ref=notes.at[sender], send_sem=note_send.at[d, c],
            recv_sem=note_recv.at[d, sender % 2], device_id={"ao": 2 * partner(chip, d) + c},
            device_id_type=MESH)

    def sibling_note(sender):
        return pltpu.make_async_remote_copy(
            src_ref=note, dst_ref=notes.at[sender], send_sem=note_send.at[0, 0],
            recv_sem=note_recv.at[0, 0], device_id={"ao": sibling}, device_id_type=MESH)

    for d, c in peers:
        note_copy(d, c, me).start()
    sibling_note(me).start()

    fetch.wait()
    for j in range(block_total):
        b_ref[j] = raw[:, :, BLK * j:BLK * (j + 1)].reshape(b_ref.shape[1:])

    def window_of(which):
        return jnp.maximum(jnp.min(notes[pl.ds(2 * which, 2)]), 0)

    def data_copy(d, sender_core, c):
        p, i = where_of[d]
        return pltpu.make_async_remote_copy(
            src_ref=send.at[d, c], dst_ref=recvs[p].at[i, sender_core, pl.ds(HALF * c, HALF)],
            send_sem=data_send.at[d, c], recv_sem=data_recv.at[d, sender_core],
            device_id={"ao": 2 * partner(chip, d) + c}, device_id_type=MESH)

    def pass_copy(d, s, c):
        p, i = where_of[d]
        part = recvs[p].at[i, s, pl.ds(HALF * c, HALF)]
        return pltpu.make_async_remote_copy(
            src_ref=part, dst_ref=part, send_sem=pass_send.at[d, s], recv_sem=pass_recv.at[d, s],
            device_id={"ao": sibling}, device_id_type=MESH)

    for d in order:
        for c in range(2):
            note_copy(d, c, 2 * partner(chip, d) + c).wait_recv()
        low = window_of(partner(chip, d))
        for c in range(2):
            send[d, c] = b_ref[pl.ds(low + HALF * c, HALF)]
            data_copy(d, core, c).start()

    sibling_note(sibling).wait_recv()
    my_low = window_of(chip)
    p0, i0 = where_of[0]
    recvs[p0][i0, core] = b_ref[pl.ds(my_low, WINDOW)]

    def own_copy(s):
        part = recvs[p0].at[i0, s]
        return pltpu.make_async_remote_copy(
            src_ref=part, dst_ref=part, send_sem=pass_send.at[0, 0], recv_sem=pass_recv.at[0, 0],
            device_id={"ao": sibling}, device_id_type=MESH)

    own_copy(core).start()

    def pass_on(p):
        for d in phases[p]:
            for s in range(2):
                if d:
                    data_copy(d, s, core).wait_recv()
                    pass_copy(d, s, core).start()

    def multiply(p):
        for d in phases[p]:
            if d == 0:
                own_copy(1 - core).wait_recv()
            else:
                for s in range(2):
                    pass_copy(d, s, 1 - core).wait_recv()

        def tile(t):
            left = jnp.clip(pairs_ref[0, t] - my_low, 0, WINDOW - 1)
            right = jnp.clip(pairs_ref[1, t] - my_low, 0, WINDOW - 1)
            a = recvs[p][:, :, left].reshape(-1, BLK)
            b = recvs[p][:, :, right].reshape(-1, BLK)
            value = lax.dot_general(a, b, (((0,), (0,)), ((), ())), preferred_element_type=jnp.float32)
            if p:
                value = value + out_ref[t]
            if p == len(phases) - 1:
                value = jnp.where(t < count, value, 0.0)
            out_ref[t] = value

        for t in range(slots):
            tile(t)

    pass_on(0)
    for p in range(1, len(phases)):
        pass_on(p)
        multiply(p - 1)
    multiply(len(phases) - 1)

    sibling_note(me).wait_send()
    for d, c in peers:
        note_copy(d, c, me).wait_send()
    own_copy(core).wait_send()
    for d in order:
        for c in range(2):
            data_copy(d, core, c).wait_send()
            pass_copy(d, c, core).wait_send()


def shards(b_factor, tile_pairs, tile_count):
    devices = lax.axis_size("ao")
    chips = devices // 2
    occ_local, auxiliary, orbitals = b_factor.shape
    depth = occ_local * auxiliary
    block_total = orbitals // BLK
    slots = tile_pairs.shape[0]
    phases = phase_lists(chips)
    in_hbm = functools.partial(pltpu.with_memory_space_constraint, memory_space=pltpu.HBM)
    return pl.pallas_call(
        functools.partial(kernel, chips, phases),
        out_shape=jax.ShapeDtypeStruct((slots, BLK, BLK), jnp.float32),
        in_specs=[
            pl.BlockSpec(memory_space=pltpu.HBM),
            pl.BlockSpec(memory_space=pltpu.SMEM),
            pl.BlockSpec(memory_space=pltpu.HBM),
        ],
        out_specs=pl.BlockSpec(memory_space=pltpu.VMEM),
        scratch_shapes=[
            pltpu.SMEM((2, slots), jnp.int32),
            pltpu.VMEM(b_factor.shape, jnp.bfloat16),
            pltpu.VMEM((block_total, depth, BLK), jnp.bfloat16),
            pltpu.VMEM((1, BLK), jnp.int32),
            pltpu.VMEM((devices, 1, BLK), jnp.int32),
            pltpu.VMEM((chips, 2, HALF, depth, BLK), jnp.bfloat16),
            *[pltpu.VMEM((len(group), 2, WINDOW, depth, BLK), jnp.bfloat16) for group in phases],
            pltpu.SemaphoreType.DMA,
            pltpu.SemaphoreType.DMA,
            pltpu.SemaphoreType.DMA((chips, 2)),
            pltpu.SemaphoreType.DMA((chips, 2)),
            pltpu.SemaphoreType.DMA((chips, 2)),
            pltpu.SemaphoreType.DMA((chips, 2)),
            pltpu.SemaphoreType.DMA((chips, 2)),
            pltpu.SemaphoreType.DMA((chips, 2)),
        ],
        compiler_params=pltpu.CompilerParams(
            collective_id=0, has_side_effects=True, vmem_limit_bytes=32 * 1024 * 1024),
    )(in_hbm(tile_pairs.T), tile_count, in_hbm(b_factor))


def solution(mesh):
    in_specs = (P("ao", "groups", None), P(("groups", "ao"), None), P(("groups", "ao")))
    out_specs = P(("groups", "ao"), None, None)
    return jax.shard_map(shards, mesh=mesh, in_specs=in_specs, out_specs=out_specs, check_vma=False)
```
